32 devices in a mesh: seq: 8 (over z, core), fsdp: 4 (over y, x).
Axes of the slice: x: 2, y: 2, z: 4, core: 2. Of those that a mesh axis runs over, the one named last changes fastest.
Arguments:
- tokens: bfloat16 [3072, 2048], P('seq'), may hold values from -6 to 6
- w_query: bfloat16 [2048, 512], P('seq', 'fsdp'), may hold values from -0.125 to 0.125
- w_key: bfloat16 [2048, 512], P('seq', 'fsdp'), may hold values from -0.125 to 0.125
- w_value: bfloat16 [2048, 512], P('seq', 'fsdp'), may hold values from -0.125 to 0.125
- norm_gain: float32 [512], P('fsdp'), may hold values from 0.1 to 1.9
- block_mask: int32 [8, 3, 3], P('seq'), may hold values 0 or 1
- cotangent: bfloat16 [3072, 512], P('seq', 'fsdp'), may hold values from -6 to 6
Outputs:
- attended: bfloat16 [3072, 512], P('seq', 'fsdp')
- grad_tokens: bfloat16 [3072, 2048], P('seq', 'fsdp')
- grad_query: bfloat16 [2048, 512], P('seq', 'fsdp')
- grad_key: bfloat16 [2048, 512], P('seq', 'fsdp')
- grad_value: bfloat16 [2048, 512], P('seq', 'fsdp')
The draws below stay inside these ranges and needn't reach their ends.
All inputs are finite; a program needn't handle non-finite values. No bound on the sum of `block_mask` on one device may be relied on, other than what follows from the above.
Results may differ from the reference program's by a relative error of at most 0.035.
Values may be sent and summed in bfloat16 or wider, within the bound.
A program may use at most 64 MiB of HBM per device.

```python
import math
import jax
import jax.numpy as jnp
from jax import lax

D = 2048
HDIM = 128
BLOCK = 128
SEG = 384
NB = 3
HEADS = 4
HD = 512
TOKENS = 3072
N_SEQ = 8


def place_ends(entries, key, smallest, largest):
    spot = [jax.random.randint(jax.random.fold_in(key, axis), (), 0, length) for axis, length in enumerate(entries.shape)]
    widest = entries.shape.index(max(entries.shape))
    beside = spot[:widest] + [(spot[widest] + 1) % entries.shape[widest]] + spot[widest + 1:]
    return entries.at[tuple(spot)].set(smallest).at[tuple(beside)].set(largest)


def spiked(drawn, rng, source, target, parts, factor):
    def block_of(dim):
        return (jnp.arange(drawn.shape[dim]) // (drawn.shape[dim] // parts)).reshape((-1,) + (1,) * (drawn.ndim - 1 - dim))

    first = jax.random.permutation(rng, parts)[block_of(target)]
    other_side = (block_of(target) + parts // 2) % parts
    return jnp.where((block_of(source) == first) | (block_of(source) == other_side), factor * drawn, drawn)


def level_of(rng, dims, pieces, smallest, high):
    def one(axis_at, blocks):
        draws = jax.random.uniform(jax.random.fold_in(jax.random.fold_in(rng, 6), axis_at), (blocks,), jnp.float32, smallest / len(pieces), high / len(pieces))
        return jnp.repeat(jnp.exp(draws), dims[axis_at] // blocks).reshape((-1,) + (1,) * (len(dims) - axis_at - 1))

    factor_of = one(*pieces[0])
    for cut in pieces[1:]:
        factor_of = factor_of * one(*cut)
    return factor_of


def gaussian(key, dims, spread, most, cuts=(), kind=jnp.bfloat16):
    gain = level_of(key, dims, cuts, -0.22, 0.18) if cuts else 1.0
    array = jax.random.normal(key, dims, jnp.float32) * spread * gain
    return jnp.minimum(jnp.maximum(array, -most), most).astype(kind)


def gaussian_with(key, dims, spread, limit, shards, heavy, held_as=jnp.bfloat16):
    entries = spread * jax.random.normal(key, dims, jnp.float32)
    if shards:
        entries = entries * level_of(key, dims, shards, -0.22, 0.18)
    return jnp.clip(spiked(entries, jax.random.fold_in(key, 3), *heavy), -limit, limit).astype(held_as)


def setup_inputs(seed: int = 0) -> dict:
    splits = jax.random.split(jax.random.key(seed), 8)
    tokens = gaussian_with(splits[0], (TOKENS, D), 1.0, 6.0, ((0, 8),), (0, 1, 8, 2.0))
    w_query = gaussian(splits[1], (D, HD), D ** -0.5, 0.125, ((0, 8), (1, 4)))
    w_key = gaussian(splits[2], (D, HD), D ** -0.5, 0.125, ((0, 8), (1, 4)))
    w_value = gaussian(splits[3], (D, HD), D ** -0.5, 0.125, ((0, 8), (1, 4)))
    norm_gain = jnp.clip(1.0 + 0.18 * jax.random.normal(splits[4], (HD,), jnp.float32), 0.1, 1.9)
    block_mask = place_ends((jax.random.randint(splits[5], (N_SEQ, NB, NB), 0, 2) < 1).astype(jnp.int32), jax.random.fold_in(splits[5], 1), 0, 1)
    cotangent = gaussian(splits[6], (TOKENS, HD), 1.0, 6.0, ((0, 8), (1, 4)))
    return dict(tokens=tokens, w_query=w_query, w_key=w_key, w_value=w_value, norm_gain=norm_gain, block_mask=block_mask, cotangent=cotangent)


EPSILON = 1e-06
EXACT = lax.Precision.HIGHEST

def rounded(value):
    return lax.optimization_barrier(value.astype(jnp.bfloat16))

def widened(value):
    return value.astype(jnp.float32)

def allowed_pairs(pattern):
    positions = jnp.arange(SEG)
    block_ids = positions // BLOCK
    selector = (block_ids[:, None] == jnp.arange(NB)[None, :]).astype(jnp.float32)
    spread_out = jnp.dot(jnp.dot(selector, pattern.astype(jnp.float32), precision=EXACT), selector.T, precision=EXACT)
    same_block = (block_ids[:, None] == block_ids[None, :]) & (positions[None, :] <= positions[:, None])
    earlier_block = (block_ids[None, :] < block_ids[:, None]) & (spread_out > 0.5)
    return same_block | earlier_block

def reference(tokens, w_query, w_key, w_value, norm_gain, block_mask, cotangent):
    weight_cat = jnp.concatenate([w_query, w_key, w_value], axis=1)
    projected = rounded(jnp.dot(widened(tokens), widened(weight_cat), precision=EXACT))
    queries = projected[:, :HD].reshape(N_SEQ, SEG, HEADS, HDIM)
    key_heads = projected[:, HD:2 * HD].reshape(N_SEQ, SEG, HEADS, HDIM)
    value_heads = projected[:, 2 * HD:].reshape(N_SEQ, SEG, HEADS, HDIM)
    increment = jnp.einsum('cthd,cthe->chde', widened(key_heads), widened(value_heads), precision=EXACT)
    running = jnp.cumsum(increment, axis=0)
    state = jnp.concatenate([jnp.zeros_like(increment[:1]), running[:-1]], axis=0)
    gain_heads = norm_gain.reshape(HEADS, HDIM)
    cot_heads = cotangent.reshape(N_SEQ, SEG, HEADS, HDIM)

    def forward_shard(items):
        query_part, key_part, value_part, state_part, pattern, cot_part = items
        allowed = allowed_pairs(pattern)
        state_low = widened(rounded(state_part))
        scores = jnp.einsum('shd,thd->hst', widened(query_part), widened(key_part), precision=EXACT)
        weights = widened(rounded(jnp.where(allowed[None], scores, 0.0)))
        mixed = jnp.einsum('shd,hde->she', widened(query_part), state_low, precision=EXACT)
        mixed = mixed + jnp.einsum('hst,the->she', weights, widened(value_part), precision=EXACT)
        scale = lax.rsqrt(lax.optimization_barrier(jnp.mean(mixed * mixed, axis=-1, keepdims=True)) + EPSILON)
        normed = mixed * scale
        attended = rounded(normed * gain_heads)
        given = widened(cot_part) * gain_heads
        d_mixed = rounded(scale * (given - normed * lax.optimization_barrier(jnp.mean(given * normed, axis=-1, keepdims=True))))
        d_state = jnp.einsum('shd,she->hde', widened(query_part), widened(d_mixed), precision=EXACT)
        return (attended, d_mixed, d_state)
    attended, d_mixed, d_state = lax.map(forward_shard, (queries, key_heads, value_heads, state, block_mask, cot_heads))
    behind = jnp.cumsum(d_state[::-1], axis=0)[::-1]
    later = jnp.concatenate([behind[1:], jnp.zeros_like(d_state[:1])], axis=0)

    def backward_shard(items):
        query_part, key_part, value_part, state_part, later_part, pattern, dmix_part = items
        allowed = allowed_pairs(pattern)
        state_low = widened(rounded(state_part))
        later_low = widened(rounded(later_part))
        query_wide = widened(query_part)
        key_wide = widened(key_part)
        value_wide = widened(value_part)
        dmix_wide = widened(dmix_part)
        scores = jnp.einsum('shd,thd->hst', query_wide, key_wide, precision=EXACT)
        weights = widened(rounded(jnp.where(allowed[None], scores, 0.0)))
        d_scores = jnp.einsum('she,the->hst', dmix_wide, value_wide, precision=EXACT)
        d_weights = widened(rounded(jnp.where(allowed[None], d_scores, 0.0)))
        d_queries = jnp.einsum('she,hde->shd', dmix_wide, state_low, precision=EXACT)
        d_queries = d_queries + jnp.einsum('hst,thd->shd', d_weights, key_wide, precision=EXACT)
        d_keys = jnp.einsum('hst,shd->thd', d_weights, query_wide, precision=EXACT)
        d_keys = d_keys + jnp.einsum('the,hde->thd', value_wide, later_low, precision=EXACT)
        d_values = jnp.einsum('hst,she->the', weights, dmix_wide, precision=EXACT)
        d_values = d_values + jnp.einsum('thd,hde->the', key_wide, later_low, precision=EXACT)
        return (rounded(d_queries), rounded(d_keys), rounded(d_values))
    d_queries, d_keys, d_values = lax.map(backward_shard, (queries, key_heads, value_heads, state, later, block_mask, d_mixed))
    grad_flat = [part.reshape(TOKENS, HEADS, HDIM) for part in (d_queries, d_keys, d_values)]
    grad_by_head = jnp.concatenate([jnp.transpose(part, (1, 0, 2)) for part in grad_flat], axis=2)
    weight_by_head = jnp.concatenate([jnp.transpose(part.reshape(D, HEADS, HDIM), (1, 0, 2)) for part in (w_query, w_key, w_value)], axis=2)

    def add_head(total, items):
        grad_head, weight_head = items
        term = jnp.dot(widened(grad_head), widened(weight_head).T, precision=EXACT)
        return (total + widened(rounded(term)), None)
    input_total, unused = lax.scan(add_head, jnp.zeros((TOKENS, D), jnp.float32), (grad_by_head, weight_by_head))
    grad_tokens = input_total.astype(jnp.bfloat16)
    grad_cat = jnp.concatenate([part.reshape(TOKENS, HD) for part in grad_flat], axis=1).reshape(N_SEQ, SEG, 3 * HD)

    def add_shard(total, items):
        token_part, grad_part = items
        term = jnp.dot(widened(token_part).T, widened(grad_part), precision=EXACT)
        return (total + widened(rounded(term)), None)
    weight_total, unused_two = lax.scan(add_shard, jnp.zeros((D, 3 * HD), jnp.float32), (tokens.reshape(N_SEQ, SEG, D), grad_cat))
    weight_total = (weight_total * (1.0 / math.sqrt(TOKENS))).astype(jnp.bfloat16)
    return (attended.reshape(TOKENS, HD), grad_tokens, weight_total[:, :HD], weight_total[:, HD:2 * HD], weight_total[:, 2 * HD:])
```

```python
import functools
import math

import jax
import jax.numpy as jnp
from jax import lax
from jax.experimental import pallas as pl
from jax.experimental.pallas import tpu as pltpu
from jax.sharding import PartitionSpec as P

HDIM = 128
BLOCK = 128
NB = 3
EPSILON = 1e-06
MESH = pl.DeviceIdType.MESH
BF = jnp.bfloat16
F32 = jnp.float32


def mm(a, b):
    return jnp.dot(a, b, preferred_element_type=F32)


def mm_nt(a, b):
    return lax.dot_general(a, b, (((1,), (1,)), ((), ())), preferred_element_type=F32)


def mm_tn(a, b):
    return lax.dot_general(a, b, (((0,), (0,)), ((), ())), preferred_element_type=F32)


def kernel(
    nz, nf,
    tok_hbm, wq_hbm, wk_hbm, wv_hbm, gain_ref, mask_ref, cot_ref,
    att_ref, gt_ref, gq_ref, gk_ref, gv_ref,
    tok, tok_t, wfull, woth, allow,
    inc_out, inc_in, inc_pair, tot_out, tot_in, run,
    dst_out, dst_in, dst_pair, dtot_out, dtot_in, drun,
    gq_own, gkv_own, gq_oth, gkv_oth,
    psq, prq, csq, crq, clq, mineq,
    psk, prk, csk, crk, clk, minek,
    load_sem, w_rs, w_rr, w_ls, w_lr, w_ps, w_pr, wo_s, wo_r, wop_s, wop_r,
    st_s, st_r, stp, tp, ds_s, ds_r, dsp, dtp,
    gq_s, gq_r, gkv_s, gkv_r,
    pq_s, pq_r, cq_s, cq_r, lq_s, lq_r,
    pk_s, pk_r, ck_s, ck_r, lk_s, lk_r,
):
    me = lax.axis_index("seq")
    f = lax.axis_index("fsdp")
    z = me // 2
    k = me - 2 * z
    other = 2 * z + 1 - k
    depth = wq_hbm.shape[0]
    seg = tok.shape[0]

    def rcopy(src, dst, ss, rs, to_seq, to_f):
        return pltpu.make_async_remote_copy(
            src_ref=src, dst_ref=dst, send_sem=ss, recv_sem=rs,
            device_id=(to_seq, to_f), device_id_type=MESH,
        )

    def rows_of(index):
        return pl.ds(pl.multiple_of(index * depth, depth), depth)

    loads = [
        pltpu.make_async_copy(w, wfull.at[rows_of(me), pl.ds(i * HDIM, HDIM)], load_sem.at[i])
        for i, w in enumerate((wq_hbm, wk_hbm, wv_hbm))
    ]
    loads.append(pltpu.make_async_copy(tok_hbm, tok, load_sem.at[3]))
    for c in loads:
        c.start()

    barrier = pltpu.get_barrier_semaphore()
    for t in range(1, nz):
        pl.semaphore_signal(
            barrier, inc=1, device_id=(2 * lax.rem(z + t, nz) + k, f), device_id_type=MESH
        )
    pl.semaphore_signal(barrier, inc=1, device_id=(other, f), device_id_type=MESH)
    for t in range(1, nf):
        pl.semaphore_signal(
            barrier, inc=1, device_id=(me, lax.rem(f + t, nf)), device_id_type=MESH
        )
    for c in loads[:3]:
        c.wait()
    pl.semaphore_wait(barrier, nz - 1 + 1 + nf - 1)

    def w_right(s):
        r = rows_of(2 * (z - s) + k)
        return rcopy(wfull.at[r], wfull.at[r], w_rs.at[s], w_rr.at[s], 2 * (z + 1) + k, f)

    def w_left(s):
        r = rows_of(2 * (z + s) + k)
        return rcopy(wfull.at[r], wfull.at[r], w_ls.at[s], w_lr.at[s], 2 * (z - 1) + k, f)

    def w_pair(j):
        r = rows_of(2 * j + k)
        return rcopy(wfull.at[r], wfull.at[r], w_ps.at[j], w_pr.at[j], other, f)

    half = pl.ds(pl.multiple_of(k * depth, depth), depth)

    def w_across(j):
        return rcopy(
            wfull.at[rows_of(2 * j + k)], woth.at[f, half], wo_s.at[j], wo_r.at[f], me, j
        )

    def w_across_pair(j):
        return rcopy(woth.at[j, half], woth.at[j, half], wop_s.at[j], wop_r.at[j], other, f)

    def spread(j):
        w_pair(j).start()

        @pl.when(j != f)
        def _():
            w_across(j).start()

    def right_has(s):
        return (z < nz - 1) & (z >= s)

    def left_has(s):
        return (z > 0) & (z + s <= nz - 1)

    for s in range(nz - 1):
        @pl.when(right_has(s))
        def _():
            w_right(s).start()

        @pl.when(left_has(s))
        def _():
            w_left(s).start()

        if s == 0:
            spread(z)
            loads[3].wait()
            tok_t[...] = tok[...].T
            row = lax.broadcasted_iota(jnp.int32, (seg, seg), 0)
            col = lax.broadcasted_iota(jnp.int32, (seg, seg), 1)
            zero = jnp.zeros((seg, seg), F32)
            total = jnp.where(col <= row, 1.0, zero)
            for a in range(NB):
                for b in range(a):
                    inside = (
                        (row >= a * BLOCK) & (row < (a + 1) * BLOCK)
                        & (col >= b * BLOCK) & (col < (b + 1) * BLOCK)
                    )
                    m = (mask_ref[0, a, b] == 1).astype(F32)
                    total = jnp.where(inside, zero + m, total)
            allow[...] = total

        @pl.when(z - 1 - s >= 0)
        def _():
            r = rows_of(2 * (z - 1 - s) + k)
            rcopy(wfull.at[r], wfull.at[r], w_rs.at[s], w_rr.at[s], other, f).wait_recv()
            spread(z - 1 - s)

        @pl.when(z + 1 + s <= nz - 1)
        def _():
            r = rows_of(2 * (z + 1 + s) + k)
            rcopy(wfull.at[r], wfull.at[r], w_ls.at[s], w_lr.at[s], other, f).wait_recv()
            spread(z + 1 + s)

    for j in range(nz):
        r = rows_of(2 * j + 1 - k)
        rcopy(wfull.at[r], wfull.at[r], w_ps.at[j], w_pr.at[j], other, f).wait_recv()

    projected = mm(tok[...], wfull[...]).astype(BF)
    q = projected[:, :HDIM]
    key = projected[:, HDIM : 2 * HDIM]
    v = projected[:, 2 * HDIM :]

    def exchange_start(mine, out, inbox, pair_in, s_sem, r_sem, p_sem, backward):
        out[...] = mine.astype(BF)
        for t in range(1, nz):
            there = z - t if backward else z + t

            @pl.when((there >= 0) & (there < nz))
            def _():
                rcopy(
                    out, inbox.at[z], s_sem.at[t], r_sem.at[z], 2 * there + k, f
                ).start()

        @pl.when(k == (1 if backward else 0))
        def _():
            rcopy(out, pair_in, p_sem.at[0], p_sem.at[1], other, f).start()

    def exchange_wait(out, inbox, pair_in, t_out, t_in, acc, r_sem, p_sem, t_sem, backward):
        acc[...] = jnp.zeros_like(acc)
        for t in range(1, nz):
            there = z + t if backward else z - t

            @pl.when((there >= 0) & (there < nz))
            def _():
                rcopy(
                    out, inbox.at[there], p_sem.at[0], r_sem.at[there], other, f
                ).wait_recv()
                acc[...] += inbox[there].astype(F32)

        t_out[...] = acc[...].astype(BF)
        total = rcopy(t_out, t_in, t_sem.at[0], t_sem.at[1], other, f)
        total.start()

        @pl.when(k == (0 if backward else 1))
        def _():
            rcopy(out, pair_in, p_sem.at[0], p_sem.at[1], other, f).wait_recv()
            acc[...] += pair_in[...].astype(F32)

        total.wait()
        return (acc[...] + t_in[...].astype(F32)).astype(BF)

    def exchange_end(out, inbox, pair_in, s_sem, r_sem, p_sem, backward):
        for t in range(1, nz):
            there = z - t if backward else z + t

            @pl.when((there >= 0) & (there < nz))
            def _():
                rcopy(
                    out, inbox.at[z], s_sem.at[t], r_sem.at[z], 2 * there + k, f
                ).wait_send()

        @pl.when(k == (1 if backward else 0))
        def _():
            rcopy(out, pair_in, p_sem.at[0], p_sem.at[1], other, f).wait_send()

    exchange_start(mm_tn(key, v), inc_out, inc_in, inc_pair, st_s, st_r, stp, False)
    ok = allow[...]
    weights = (mm_nt(q, key) * ok).astype(BF)
    mixed = mm(weights, v)
    gain = gain_ref[...]
    given = cot_ref[...].astype(F32) * gain

    state = exchange_wait(inc_out, inc_in, inc_pair, tot_out, tot_in, run, st_r, stp, tp, False)
    mixed = mixed + mm(q, state)
    scale = lax.rsqrt(jnp.mean(mixed * mixed, axis=-1, keepdims=True) + EPSILON)
    normed = mixed * scale
    d_mixed = (
        scale * (given - normed * jnp.mean(given * normed, axis=-1, keepdims=True))
    ).astype(BF)
    exchange_start(mm_tn(q, d_mixed), dst_out, dst_in, dst_pair, ds_s, ds_r, dsp, True)
    att_ref[...] = (normed * gain).astype(BF)
    d_weights = (mm_nt(d_mixed, v) * ok).astype(BF)
    gq_own[...] = (mm_nt(d_mixed, state) + mm(d_weights, key)).astype(BF)

    def across(own, oth, s_sem, r_sem, t):
        there = lax.rem(f + t, nf)
        return rcopy(own, oth.at[f], s_sem.at[t], r_sem.at[f], me, there)

    def across_wait(own, oth, s_sem, r_sem, t):
        there = lax.rem(f + t, nf)
        rcopy(own, oth.at[there], s_sem.at[t], r_sem.at[there], other, f).wait_recv()
        return there

    def rs_start(g, ps, pr, p_s, p_r):
        grads = g[...]
        for j in range(nz):
            ps[j] = mm(tok_t[rows_of(2 * j + 1 - k)], grads).astype(BF)
            rcopy(ps.at[j], pr.at[j], p_s.at[j], p_r.at[j], other, f).start()

    def rs_mine(g, mine):
        grads = g[...]
        for j in range(nz):
            mine[j] = mm(tok_t[rows_of(2 * j + k)], grads)

    def rs_chain(ps, pr, cs, cr, cl, mine, p_s, p_r, c_s, c_r, l_s, l_r):
        for j in range(nz):
            rcopy(ps.at[j], pr.at[j], p_s.at[j], p_r.at[j], other, f).wait_recv()
            mine[j] += pr[j].astype(F32)
        for i in range(nz - 1):
            j = nz - 1 - i

            @pl.when(z < j)
            def _():
                @pl.when(z > 0)
                def _():
                    rcopy(cs.at[j], cr.at[j], c_s.at[j], c_r.at[j], other, f).wait_recv()
                    cs[j] = (mine[j] + cr[j].astype(F32)).astype(BF)

                @pl.when(z == 0)
                def _():
                    cs[j] = mine[j].astype(BF)

                rcopy(cs.at[j], cr.at[j], c_s.at[j], c_r.at[j], 2 * (z + 1) + k, f).start()

            @pl.when(z > i)
            def _():
                @pl.when(z < nz - 1)
                def _():
                    rcopy(cs.at[i], cl.at[i], l_s.at[i], l_r.at[i], other, f).wait_recv()
                    cs[i] = (mine[i] + cl[i].astype(F32)).astype(BF)

                @pl.when(z == nz - 1)
                def _():
                    cs[i] = mine[i].astype(BF)

                rcopy(cs.at[i], cl.at[i], l_s.at[i], l_r.at[i], 2 * (z - 1) + k, f).start()

    def rs_end(ps, pr, cs, cr, cl, mine, p_s, p_r, c_s, c_r, l_s, l_r):
        @pl.when(z > 0)
        def _():
            rcopy(cs.at[z], cr.at[z], c_s.at[z], c_r.at[z], other, f).wait_recv()
            mine[z] += cr[z].astype(F32)

        @pl.when(z < nz - 1)
        def _():
            rcopy(cs.at[z], cl.at[z], l_s.at[z], l_r.at[z], other, f).wait_recv()
            mine[z] += cl[z].astype(F32)

        return mine[z] * (1.0 / math.sqrt(seg * 2 * nz))

    def rs_drain(ps, pr, cs, cr, cl, mine, p_s, p_r, c_s, c_r, l_s, l_r):
        for j in range(nz):
            rcopy(ps.at[j], pr.at[j], p_s.at[j], p_r.at[j], other, f).wait_send()

            @pl.when(z < j)
            def _():
                rcopy(cs.at[j], cr.at[j], c_s.at[j], c_r.at[j], other, f).wait_send()

            @pl.when(z > j)
            def _():
                rcopy(cs.at[j], cl.at[j], l_s.at[j], l_r.at[j], other, f).wait_send()

    q_set = (psq, prq, csq, crq, clq, mineq, pq_s, pq_r, cq_s, cq_r, lq_s, lq_r)
    k_set = (psk, prk, csk, crk, clk, minek, pk_s, pk_r, ck_s, ck_r, lk_s, lk_r)

    for t in range(1, nf):
        across(gq_own, gq_oth, gq_s, gq_r, t).start()
    rs_start(gq_own, psq, prq, pq_s, pq_r)
    for t in range(1, nf):
        there = lax.rem(f + t, nf)
        rcopy(
            wfull.at[rows_of(me)], woth.at[there, half], wo_s.at[there], wo_r.at[there], other, f
        ).wait_recv()
        w_across_pair(there).start()
    d_keys = mm_tn(d_weights, q)
    d_values = mm_tn(weights, d_mixed)
    rs_mine(gq_own, mineq)

    later = exchange_wait(dst_out, dst_in, dst_pair, dtot_out, dtot_in, drun, ds_r, dsp, dtp, True)
    gkv_own[:, :HDIM] = (d_keys + mm_nt(v, later)).astype(BF)
    gkv_own[:, HDIM:] = (d_values + mm(key, later)).astype(BF)
    for t in range(1, nf):
        across(gkv_own, gkv_oth, gkv_s, gkv_r, t).start()
    rs_start(gkv_own, psk, prk, pk_s, pk_r)
    rs_chain(*q_set)
    rs_mine(gkv_own, minek)
    rs_chain(*k_set)

    mine_rows = pl.ds(pl.multiple_of(f * 2 * depth, depth), 2 * depth)
    total = mm_nt(gq_own[...], wfull[mine_rows, :HDIM])
    total = total + mm_nt(gkv_own[...], wfull[mine_rows, HDIM:])
    away = pl.ds(pl.multiple_of((1 - k) * depth, depth), depth)
    for t in range(1, nf):
        there = lax.rem(f + t, nf)
        rcopy(
            woth.at[there, away], woth.at[there, away], wop_s.at[there], wop_r.at[there], other, f
        ).wait_recv()
        across_wait(gq_own, gq_oth, gq_s, gq_r, t)
        across_wait(gkv_own, gkv_oth, gkv_s, gkv_r, t)
        total = total + mm_nt(gq_oth[there], woth[there, :, :HDIM])
        total = total + mm_nt(gkv_oth[there], woth[there, :, HDIM:])
    gt_ref[...] = total.astype(BF)

    gq_ref[...] = rs_end(*q_set).astype(BF)
    both = rs_end(*k_set)
    gk_ref[...] = both[:, :HDIM].astype(BF)
    gv_ref[...] = both[:, HDIM:].astype(BF)

    for s in range(nz - 1):
        @pl.when(right_has(s))
        def _():
            w_right(s).wait_send()

        @pl.when(left_has(s))
        def _():
            w_left(s).wait_send()

    for j in range(nz):
        w_pair(j).wait_send()

        @pl.when(f != j)
        def _():
            w_across(j).wait_send()
            w_across_pair(j).wait_send()

    exchange_end(inc_out, inc_in, inc_pair, st_s, st_r, stp, False)
    exchange_end(dst_out, dst_in, dst_pair, ds_s, ds_r, dsp, True)
    for t in range(1, nf):
        across(gq_own, gq_oth, gq_s, gq_r, t).wait_send()
        across(gkv_own, gkv_oth, gkv_s, gkv_r, t).wait_send()
    rs_drain(*q_set)
    rs_drain(*k_set)


def shards(nz, nf, tokens, w_query, w_key, w_value, norm_gain, block_mask, cotangent):
    seg, features = tokens.shape
    depth, columns = w_query.shape
    vm = pl.BlockSpec(memory_space=pltpu.VMEM)
    hbm = pl.BlockSpec(memory_space=pl.ANY)
    dma = pltpu.SemaphoreType.DMA
    wide = 3 * columns

    def buf(*shape, kind=BF):
        return pltpu.VMEM(shape, kind)

    def exchange_bufs():
        return [
            buf(HDIM, HDIM), buf(nz, HDIM, HDIM), buf(HDIM, HDIM),
            buf(HDIM, HDIM), buf(HDIM, HDIM), buf(HDIM, HDIM, kind=F32),
        ]

    def rs_bufs(width):
        return [buf(nz, depth, width) for _ in range(5)] + [buf(nz, depth, width, kind=F32)]

    one = dma((nz,))
    exchange_sems = [dma((nz,)), dma((nz,)), dma((2,)), dma((2,))]
    scratch = (
        [
            buf(seg, features), buf(features, seg), buf(features, wide),
            buf(nf, 2 * depth, wide), buf(seg, seg, kind=F32),
        ]
        + exchange_bufs() + exchange_bufs()
        + [
            buf(seg, HDIM), buf(seg, 2 * HDIM),
            buf(nf, seg, HDIM), buf(nf, seg, 2 * HDIM),
        ]
        + rs_bufs(HDIM) + rs_bufs(2 * HDIM)
        + [dma((4,)), one, one, one, one, one, one, dma((nf,)), dma((nf,)), dma((nf,)), dma((nf,))]
        + exchange_sems + exchange_sems
        + [dma((nf,))] * 4
        + [one] * 12
    )
    return pl.pallas_call(
        functools.partial(kernel, nz, nf),
        out_shape=(
            jax.ShapeDtypeStruct((seg, columns), BF),
            jax.ShapeDtypeStruct((seg, features // nf), BF),
            jax.ShapeDtypeStruct((depth, columns), BF),
            jax.ShapeDtypeStruct((depth, columns), BF),
            jax.ShapeDtypeStruct((depth, columns), BF),
        ),
        in_specs=[hbm, hbm, hbm, hbm, vm, pl.BlockSpec(memory_space=pltpu.SMEM), vm],
        out_specs=(vm,) * 5,
        scratch_shapes=scratch,
        compiler_params=pltpu.CompilerParams(
            collective_id=0, has_side_effects=True, vmem_limit_bytes=40 * 1024 * 1024
        ),
    )(
        tokens, w_query, w_key, w_value, norm_gain.reshape(1, columns), block_mask, cotangent
    )


def solution(mesh):
    nz, nf = mesh.shape["seq"] // 2, mesh.shape["fsdp"]
    assert nz == nf
    placed = (
        P("seq", None),
        P("seq", "fsdp"),
        P("seq", "fsdp"),
        P("seq", "fsdp"),
        P("fsdp"),
        P("seq", None, None),
        P("seq", "fsdp"),
    )
    return jax.shard_map(
        functools.partial(shards, nz, nf),
        mesh=mesh,
        in_specs=placed,
        out_specs=(P("seq", "fsdp"),) * 5,
        check_vma=False,
    )
```

```python
import functools
import math

import jax
import jax.numpy as jnp
from jax import lax
from jax.experimental import pallas as pl
from jax.experimental.pallas import tpu as pltpu
from jax.sharding import PartitionSpec as P

HDIM = 128
BLOCK = 128
NB = 3
EPSILON = 1e-06
MESH = pl.DeviceIdType.MESH
BF = jnp.bfloat16
F32 = jnp.float32
LIMIT = 60 * 1024 * 1024


def mm(a, b):
    return jnp.dot(a, b, preferred_element_type=F32)


def mm_nt(a, b):
    return lax.dot_general(a, b, (((1,), (1,)), ((), ())), preferred_element_type=F32)


def mm_tn(a, b):
    return lax.dot_general(a, b, (((0,), (0,)), ((), ())), preferred_element_type=F32)


def kernel(
    nz, nf,
    tok_hbm, wq_hbm, wk_hbm, wv_hbm, gain_hbm, mask_hbm, cot_hbm,
    att_ref, gt_ref, gq_ref, gk_ref, gv_ref,
    tok, tok_t, wfull, woth, allow, proj, gain_ref, mask_ref, cot_ref,
    inc_out, inc_in, inc_pair, tot_out, tot_in, run,
    dst_out, dst_in, dst_pair, dtot_out, dtot_in, drun,
    gq_own, gkv_own, gq_oth, gkv_oth,
    psq, prq, csq, crq, clq, mineq,
    psk, prk, csk, crk, clk, minek,
    load_sem, w_rs, w_rr, w_ls, w_lr, w_ps, w_pr, wo_s, wo_r, wop_s, wop_r,
    st_s, st_r, stp, tp, ds_s, ds_r, dsp, dtp,
    gq_s, gq_r, gkv_s, gkv_r,
    pq_s, pq_r, cq_s, cq_r, lq_s, lq_r,
    pk_s, pk_r, ck_s, ck_r, lk_s, lk_r,
):
    me = lax.axis_index("seq")
    f = lax.axis_index("fsdp")
    z = me // 2
    k = me - 2 * z
    other = 2 * z + 1 - k
    depth = wq_hbm.shape[0]
    seg = tok.shape[0]

    def rcopy(src, dst, ss, rs, to_seq, to_f):
        return pltpu.make_async_remote_copy(
            src_ref=src, dst_ref=dst, send_sem=ss, recv_sem=rs,
            device_id=(to_seq, to_f), device_id_type=MESH,
        )

    def rows_of(index):
        return pl.ds(pl.multiple_of(index * depth, depth), depth)

    loads = [
        pltpu.make_async_copy(w, wfull.at[rows_of(me), pl.ds(i * HDIM, HDIM)], load_sem.at[i])
        for i, w in enumerate((wq_hbm, wk_hbm, wv_hbm))
    ]
    loads.append(pltpu.make_async_copy(tok_hbm, tok, load_sem.at[3]))
    loads.append(pltpu.make_async_copy(mask_hbm, mask_ref, load_sem.at[4]))
    loads.append(pltpu.make_async_copy(gain_hbm, gain_ref, load_sem.at[5]))
    loads.append(pltpu.make_async_copy(cot_hbm, cot_ref, load_sem.at[6]))
    for c in loads:
        c.start()

    barrier = pltpu.get_barrier_semaphore()
    for t in range(1, nz):
        pl.semaphore_signal(
            barrier, inc=1, device_id=(2 * lax.rem(z + t, nz) + k, f), device_id_type=MESH
        )
    pl.semaphore_signal(barrier, inc=1, device_id=(other, f), device_id_type=MESH)
    for t in range(1, nf):
        pl.semaphore_signal(
            barrier, inc=1, device_id=(me, lax.rem(f + t, nf)), device_id_type=MESH
        )
    for c in loads[:3]:
        c.wait()
    pl.semaphore_wait(barrier, nz - 1 + 1 + nf - 1)

    part = depth // 2

    def part_of(index, u):
        return pl.ds(pl.multiple_of(index * depth + u * part, part), part)

    def w_right(s, u):
        r = part_of(2 * (z - s) + k, u)
        n = 2 * s + u
        return rcopy(wfull.at[r], wfull.at[r], w_rs.at[n], w_rr.at[n], 2 * (z + 1) + k, f)

    def w_left(s, u):
        r = part_of(2 * (z + s) + k, u)
        n = 2 * s + u
        return rcopy(wfull.at[r], wfull.at[r], w_ls.at[n], w_lr.at[n], 2 * (z - 1) + k, f)

    def w_pair(j, u):
        r = part_of(2 * j + k, u)
        n = 2 * j + u
        return rcopy(wfull.at[r], wfull.at[r], w_ps.at[n], w_pr.at[n], other, f)

    half = pl.ds(pl.multiple_of(k * depth, depth), depth)

    def w_across(j):
        return rcopy(
            wfull.at[rows_of(2 * j + k)], woth.at[f, half], wo_s.at[j], wo_r.at[f], me, j
        )

    def w_across_pair(j):
        return rcopy(woth.at[j, half], woth.at[j, half], wop_s.at[j], wop_r.at[j], other, f)

    def send_across(j):
        @pl.when(j != f)
        def _():
            w_across(j).start()

    def add_pair(j):
        for u in range(2):
            r = part_of(2 * j + 1 - k, u)
            n = 2 * j + u
            rcopy(wfull.at[r], wfull.at[r], w_ps.at[n], w_pr.at[n], other, f).wait_recv()
        span = pl.ds(pl.multiple_of(j * 2 * depth, 2 * depth), 2 * depth)
        proj[...] += mm(tok[:, span], wfull[span])

    def right_has(s):
        return (z < nz - 1) & (z >= s)

    def left_has(s):
        return (z > 0) & (z + s <= nz - 1)

    for u in range(2):
        @pl.when(z < nz - 1)
        def _():
            w_right(0, u).start()

        @pl.when(z > 0)
        def _():
            w_left(0, u).start()

    for u in range(2):
        w_pair(z, u).start()
    send_across(z)
    for c in loads[3:]:
        c.wait()
    tok_t[...] = tok[...].T
    row = lax.broadcasted_iota(jnp.int32, (seg, seg), 0)
    col = lax.broadcasted_iota(jnp.int32, (seg, seg), 1)
    zero = jnp.zeros((seg, seg), F32)
    total = jnp.where(col <= row, 1.0, zero)
    for a in range(NB):
        for b in range(a):
            inside = (
                (row >= a * BLOCK) & (row < (a + 1) * BLOCK)
                & (col >= b * BLOCK) & (col < (b + 1) * BLOCK)
            )
            m = jnp.where(mask_ref[a, 0:1, b : b + 1] == 1, 1.0, 0.0)
            total = jnp.where(inside, m, total)
    allow[...] = total
    proj[...] = jnp.zeros_like(proj)

    for s in range(nz - 1):
        for u in range(2):
            n = 2 * s + u

            @pl.when(z - 1 - s >= 0)
            def _():
                r = part_of(2 * (z - 1 - s) + k, u)
                rcopy(wfull.at[r], wfull.at[r], w_rs.at[n], w_rr.at[n], other, f).wait_recv()
                if s < nz - 2:
                    @pl.when(z < nz - 1)
                    def _():
                        w_right(s + 1, u).start()

                w_pair(z - 1 - s, u).start()
                if u == 1:
                    send_across(z - 1 - s)

            @pl.when(z + 1 + s <= nz - 1)
            def _():
                r = part_of(2 * (z + 1 + s) + k, u)
                rcopy(wfull.at[r], wfull.at[r], w_ls.at[n], w_lr.at[n], other, f).wait_recv()
                if s < nz - 2:
                    @pl.when(z > 0)
                    def _():
                        w_left(s + 1, u).start()

                w_pair(z + 1 + s, u).start()
                if u == 1:
                    send_across(z + 1 + s)

        if s == 0:
            add_pair(z)
        else:
            @pl.when(z - s >= 0)
            def _():
                add_pair(z - s)

            @pl.when(z + s <= nz - 1)
            def _():
                add_pair(z + s)

    @pl.when(z == nz - 1)
    def _():
        add_pair(0)

    @pl.when(z == 0)
    def _():
        add_pair(nz - 1)

    projected = proj[...].astype(BF)
    q = projected[:, :HDIM]
    key = projected[:, HDIM : 2 * HDIM]
    v = projected[:, 2 * HDIM :]

    def exchange_start(mine, out, inbox, pair_in, s_sem, r_sem, p_sem, backward):
        out[...] = mine.astype(BF)
        for t in range(1, nz):
            there = z - t if backward else z + t

            @pl.when((there >= 0) & (there < nz))
            def _():
                rcopy(
                    out, inbox.at[z], s_sem.at[t], r_sem.at[z], 2 * there + k, f
                ).start()

        @pl.when(k == (1 if backward else 0))
        def _():
            rcopy(out, pair_in, p_sem.at[0], p_sem.at[1], other, f).start()

    def exchange_wait(out, inbox, pair_in, t_out, t_in, acc, r_sem, p_sem, t_sem, backward):
        acc[...] = jnp.zeros_like(acc)
        for t in range(1, nz):
            there = z + t if backward else z - t

            @pl.when((there >= 0) & (there < nz))
            def _():
                rcopy(
                    out, inbox.at[there], p_sem.at[0], r_sem.at[there], other, f
                ).wait_recv()
                acc[...] += inbox[there].astype(F32)

        t_out[...] = acc[...].astype(BF)
        total = rcopy(t_out, t_in, t_sem.at[0], t_sem.at[1], other, f)
        total.start()

        @pl.when(k == (0 if backward else 1))
        def _():
            rcopy(out, pair_in, p_sem.at[0], p_sem.at[1], other, f).wait_recv()
            acc[...] += pair_in[...].astype(F32)

        total.wait()
        return (acc[...] + t_in[...].astype(F32)).astype(BF)

    def exchange_end(out, inbox, pair_in, s_sem, r_sem, p_sem, backward):
        for t in range(1, nz):
            there = z - t if backward else z + t

            @pl.when((there >= 0) & (there < nz))
            def _():
                rcopy(
                    out, inbox.at[z], s_sem.at[t], r_sem.at[z], 2 * there + k, f
                ).wait_send()

        @pl.when(k == (1 if backward else 0))
        def _():
            rcopy(out, pair_in, p_sem.at[0], p_sem.at[1], other, f).wait_send()

    exchange_start(mm_tn(key, v), inc_out, inc_in, inc_pair, st_s, st_r, stp, False)
    ok = allow[...]
    weights = (mm_nt(q, key) * ok).astype(BF)
    mixed = mm(weights, v)
    gain = gain_ref[...]
    given = cot_ref[...].astype(F32) * gain

    state = exchange_wait(inc_out, inc_in, inc_pair, tot_out, tot_in, run, st_r, stp, tp, False)
    mixed = mixed + mm(q, state)
    scale = lax.rsqrt(jnp.mean(mixed * mixed, axis=-1, keepdims=True) + EPSILON)
    normed = mixed * scale
    d_mixed = (
        scale * (given - normed * jnp.mean(given * normed, axis=-1, keepdims=True))
    ).astype(BF)
    exchange_start(mm_tn(q, d_mixed), dst_out, dst_in, dst_pair, ds_s, ds_r, dsp, True)
    att_ref[...] = (normed * gain).astype(BF)
    d_weights = (mm_nt(d_mixed, v) * ok).astype(BF)
    gq_own[...] = (mm_nt(d_mixed, state) + mm(d_weights, key)).astype(BF)

    def across(own, oth, s_sem, r_sem, t):
        there = lax.rem(f + t, nf)
        return rcopy(own, oth.at[f], s_sem.at[t], r_sem.at[f], me, there)

    def across_wait(own, oth, s_sem, r_sem, t):
        there = lax.rem(f + t, nf)
        rcopy(own, oth.at[there], s_sem.at[t], r_sem.at[there], other, f).wait_recv()
        return there

    order = []
    for i in range(nz):
        for j in (nz - 1 - i, i):
            if j not in order:
                order.append(j)

    def rs_start(g, ps, pr, p_s, p_r):
        grads = g[...]
        for j in order:
            ps[j] = mm(tok_t[rows_of(2 * j + 1 - k)], grads).astype(BF)
            rcopy(ps.at[j], pr.at[j], p_s.at[j], p_r.at[j], other, f).start()

    def rs_mine(g, mine):
        grads = g[...]
        for j in order:
            mine[j] = mm(tok_t[rows_of(2 * j + k)], grads)

    def rs_ends(ps, pr, cs, cr, cl, mine, p_s, p_r, c_s, c_r, l_s, l_r):
        @pl.when(z == 0)
        def _():
            for j in range(nz - 1, 0, -1):
                rcopy(ps.at[j], pr.at[j], p_s.at[j], p_r.at[j], other, f).wait_recv()
                cs[j] = (mine[j] + pr[j].astype(F32)).astype(BF)
                rcopy(cs.at[j], cr.at[j], c_s.at[j], c_r.at[j], 2 + k, f).start()

        @pl.when(z == nz - 1)
        def _():
            for j in range(nz - 1):
                rcopy(ps.at[j], pr.at[j], p_s.at[j], p_r.at[j], other, f).wait_recv()
                cs[j] = (mine[j] + pr[j].astype(F32)).astype(BF)
                rcopy(cs.at[j], cl.at[j], l_s.at[j], l_r.at[j], 2 * (nz - 2) + k, f).start()

    def rs_inner(ps, pr, cs, cr, cl, mine, p_s, p_r, c_s, c_r, l_s, l_r):
        for i in range(nz - 1):
            j = nz - 1 - i

            @pl.when((z < j) & (z > 0))
            def _():
                rcopy(ps.at[j], pr.at[j], p_s.at[j], p_r.at[j], other, f).wait_recv()
                mine[j] += pr[j].astype(F32)
                rcopy(cs.at[j], cr.at[j], c_s.at[j], c_r.at[j], other, f).wait_recv()
                cs[j] = (mine[j] + cr[j].astype(F32)).astype(BF)
                rcopy(cs.at[j], cr.at[j], c_s.at[j], c_r.at[j], 2 * (z + 1) + k, f).start()

            @pl.when((z > i) & (z < nz - 1))
            def _():
                rcopy(ps.at[i], pr.at[i], p_s.at[i], p_r.at[i], other, f).wait_recv()
                mine[i] += pr[i].astype(F32)
                rcopy(cs.at[i], cl.at[i], l_s.at[i], l_r.at[i], other, f).wait_recv()
                cs[i] = (mine[i] + cl[i].astype(F32)).astype(BF)
                rcopy(cs.at[i], cl.at[i], l_s.at[i], l_r.at[i], 2 * (z - 1) + k, f).start()

    def rs_end(ps, pr, cs, cr, cl, mine, p_s, p_r, c_s, c_r, l_s, l_r):
        rcopy(ps.at[z], pr.at[z], p_s.at[z], p_r.at[z], other, f).wait_recv()
        mine[z] += pr[z].astype(F32)

        @pl.when(z > 0)
        def _():
            rcopy(cs.at[z], cr.at[z], c_s.at[z], c_r.at[z], other, f).wait_recv()
            mine[z] += cr[z].astype(F32)

        @pl.when(z < nz - 1)
        def _():
            rcopy(cs.at[z], cl.at[z], l_s.at[z], l_r.at[z], other, f).wait_recv()
            mine[z] += cl[z].astype(F32)

        return mine[z] * (1.0 / math.sqrt(seg * 2 * nz))

    def rs_drain(ps, pr, cs, cr, cl, mine, p_s, p_r, c_s, c_r, l_s, l_r):
        for j in range(nz):
            rcopy(ps.at[j], pr.at[j], p_s.at[j], p_r.at[j], other, f).wait_send()

            @pl.when(z < j)
            def _():
                rcopy(cs.at[j], cr.at[j], c_s.at[j], c_r.at[j], other, f).wait_send()

            @pl.when(z > j)
            def _():
                rcopy(cs.at[j], cl.at[j], l_s.at[j], l_r.at[j], other, f).wait_send()

    q_set = (psq, prq, csq, crq, clq, mineq, pq_s, pq_r, cq_s, cq_r, lq_s, lq_r)
    k_set = (psk, prk, csk, crk, clk, minek, pk_s, pk_r, ck_s, ck_r, lk_s, lk_r)

    for t in range(1, nf):
        across(gq_own, gq_oth, gq_s, gq_r, t).start()
    rs_start(gq_own, psq, prq, pq_s, pq_r)
    for t in range(1, nf):
        there = lax.rem(f + t, nf)
        rcopy(
            wfull.at[rows_of(me)], woth.at[there, half], wo_s.at[there], wo_r.at[there], other, f
        ).wait_recv()
        w_across_pair(there).start()
    d_keys = mm_tn(d_weights, q)
    d_values = mm_tn(weights, d_mixed)
    rs_mine(gq_own, mineq)
    rs_ends(*q_set)

    later = exchange_wait(dst_out, dst_in, dst_pair, dtot_out, dtot_in, drun, ds_r, dsp, dtp, True)
    gkv_own[:, :HDIM] = (d_keys + mm_nt(v, later)).astype(BF)
    gkv_own[:, HDIM:] = (d_values + mm(key, later)).astype(BF)
    for t in range(1, nf):
        across(gkv_own, gkv_oth, gkv_s, gkv_r, t).start()
    rs_start(gkv_own, psk, prk, pk_s, pk_r)
    rs_mine(gkv_own, minek)
    rs_inner(*q_set)
    rs_ends(*k_set)
    rs_inner(*k_set)

    mine_rows = pl.ds(pl.multiple_of(f * 2 * depth, depth), 2 * depth)
    total = mm_nt(gq_own[...], wfull[mine_rows, :HDIM])
    total = total + mm_nt(gkv_own[...], wfull[mine_rows, HDIM:])
    away = pl.ds(pl.multiple_of((1 - k) * depth, depth), depth)
    for t in range(1, nf):
        there = lax.rem(f + t, nf)
        rcopy(
            woth.at[there, away], woth.at[there, away], wop_s.at[there], wop_r.at[there], other, f
        ).wait_recv()
        across_wait(gq_own, gq_oth, gq_s, gq_r, t)
        across_wait(gkv_own, gkv_oth, gkv_s, gkv_r, t)
        total = total + mm_nt(gq_oth[there], woth[there, :, :HDIM])
        total = total + mm_nt(gkv_oth[there], woth[there, :, HDIM:])
    gt_ref[...] = total.astype(BF)

    gq_ref[...] = rs_end(*q_set).astype(BF)
    both = rs_end(*k_set)
    gk_ref[...] = both[:, :HDIM].astype(BF)
    gv_ref[...] = both[:, HDIM:].astype(BF)

    for s in range(nz - 1):
        @pl.when(right_has(s))
        def _():
            for u in range(2):
                w_right(s, u).wait_send()

        @pl.when(left_has(s))
        def _():
            for u in range(2):
                w_left(s, u).wait_send()

    for j in range(nz):
        for u in range(2):
            w_pair(j, u).wait_send()

        @pl.when(f != j)
        def _():
            w_across(j).wait_send()
            w_across_pair(j).wait_send()

    exchange_end(inc_out, inc_in, inc_pair, st_s, st_r, stp, False)
    exchange_end(dst_out, dst_in, dst_pair, ds_s, ds_r, dsp, True)
    for t in range(1, nf):
        across(gq_own, gq_oth, gq_s, gq_r, t).wait_send()
        across(gkv_own, gkv_oth, gkv_s, gkv_r, t).wait_send()
    rs_drain(*q_set)
    rs_drain(*k_set)


def hand_over(*refs):
    sems = refs[10]
    copies = [pltpu.make_async_copy(refs[i], refs[5 + i], sems.at[i]) for i in range(5)]
    for c in copies:
        c.start()
    for c in copies:
        c.wait()


def shards(nz, nf, tokens, w_query, w_key, w_value, norm_gain, block_mask, cotangent):
    seg, features = tokens.shape
    depth, columns = w_query.shape
    vm = pl.BlockSpec(memory_space=pltpu.VMEM)
    hbm = pl.BlockSpec(memory_space=pl.ANY)
    dma = pltpu.SemaphoreType.DMA
    wide = 3 * columns

    def buf(*shape, kind=BF):
        return pltpu.VMEM(shape, kind)

    def exchange_bufs():
        return [
            buf(HDIM, HDIM), buf(nz, HDIM, HDIM), buf(HDIM, HDIM),
            buf(HDIM, HDIM), buf(HDIM, HDIM), buf(HDIM, HDIM, kind=F32),
        ]

    def rs_bufs(width):
        return [buf(nz, depth, width) for _ in range(5)] + [buf(nz, depth, width, kind=F32)]

    one = dma((nz,))
    exchange_sems = [dma((nz,)), dma((nz,)), dma((2,)), dma((2,))]
    scratch = (
        [
            buf(seg, features), buf(features, seg), buf(features, wide),
            buf(nf, 2 * depth, wide), buf(seg, seg, kind=F32),
            buf(seg, wide, kind=F32), buf(1, columns, kind=F32),
            buf(NB, 1, NB, kind=jnp.int32), buf(seg, columns),
        ]
        + exchange_bufs() + exchange_bufs()
        + [
            buf(seg, HDIM), buf(seg, 2 * HDIM),
            buf(nf, seg, HDIM), buf(nf, seg, 2 * HDIM),
        ]
        + rs_bufs(HDIM) + rs_bufs(2 * HDIM)
        + [dma((7,))] + [dma((2 * nz,))] * 6 + [ dma((nf,)), dma((nf,)), dma((nf,)), dma((nf,))]
        + exchange_sems + exchange_sems
        + [dma((nf,))] * 4
        + [one] * 12
    )
    results = pl.pallas_call(
        functools.partial(kernel, nz, nf),
        out_shape=(
            jax.ShapeDtypeStruct((seg, columns), BF),
            jax.ShapeDtypeStruct((seg, features // nf), BF),
            jax.ShapeDtypeStruct((depth, columns), BF),
            jax.ShapeDtypeStruct((depth, columns), BF),
            jax.ShapeDtypeStruct((depth, columns), BF),
        ),
        in_specs=[hbm] * 7,
        out_specs=(vm,) * 5,
        scratch_shapes=scratch,
        compiler_params=pltpu.CompilerParams(
            collective_id=0, has_side_effects=True, vmem_limit_bytes=LIMIT
        ),
    )(
        tokens, w_query, w_key, w_value, norm_gain.reshape(1, columns),
        jnp.transpose(block_mask, (1, 0, 2)), cotangent
    )
    return pl.pallas_call(
        hand_over,
        out_shape=tuple(jax.ShapeDtypeStruct(r.shape, r.dtype) for r in results),
        in_specs=[hbm] * 5,
        out_specs=(hbm,) * 5,
        scratch_shapes=[dma((5,))],
    )(*results)


def solution(mesh):
    nz, nf = mesh.shape["seq"] // 2, mesh.shape["fsdp"]
    assert nz == nf
    placed = (
        P("seq", None),
        P("seq", "fsdp"),
        P("seq", "fsdp"),
        P("seq", "fsdp"),
        P("fsdp"),
        P("seq", None, None),
        P("seq", "fsdp"),
    )
    return jax.shard_map(
        functools.partial(shards, nz, nf),
        mesh=mesh,
        in_specs=placed,
        out_specs=(P("seq", "fsdp"),) * 5,
        check_vma=False,
    )
```

```python
import functools
import math

import jax
import jax.numpy as jnp
from jax import lax
from jax.experimental import pallas as pl
from jax.experimental.pallas import tpu as pltpu
from jax.sharding import PartitionSpec as P

HDIM = 128
BLOCK = 128
NB = 3
EPSILON = 1e-06
MESH = pl.DeviceIdType.MESH
BF = jnp.bfloat16
F32 = jnp.float32
LIMIT = 60 * 1024 * 1024


def mm(a, b):
    return jnp.dot(a, b, preferred_element_type=F32)


def mm_nt(a, b):
    return lax.dot_general(a, b, (((1,), (1,)), ((), ())), preferred_element_type=F32)


def mm_tn(a, b):
    return lax.dot_general(a, b, (((0,), (0,)), ((), ())), preferred_element_type=F32)


def kernel(
    nz, nf,
    tok_hbm, wq_hbm, wk_hbm, wv_hbm, gain_hbm, mask_hbm, cot_hbm,
    att_ref, gt_ref, gq_ref, gk_ref, gv_ref,
    tok, tok_t, wfull, woth, allow, proj, gain_ref, mask_ref, cot_ref,
    inc_out, inc_in, inc_pair, tot_out, tot_in, run,
    dst_out, dst_in, dst_pair, dtot_out, dtot_in, drun,
    gq_own, gkv_own, gq_oth, gkv_oth,
    psq, prq, csq, crq, clq, mineq,
    psk, prk, csk, crk, clk, minek,
    load_sem, w_rs, w_rr, w_ls, w_lr, w_ps, w_pr, wo_s, wo_r, wop_s, wop_r,
    st_s, st_r, stp, tp, ds_s, ds_r, dsp, dtp,
    gq_s, gq_r, gkv_s, gkv_r,
    pq_s, pq_r, cq_s, cq_r, lq_s, lq_r,
    pk_s, pk_r, ck_s, ck_r, lk_s, lk_r,
):
    me = lax.axis_index("seq")
    f = lax.axis_index("fsdp")
    z = me // 2
    k = me - 2 * z
    other = 2 * z + 1 - k
    depth = wq_hbm.shape[0]
    seg = tok.shape[0]

    def rcopy(src, dst, ss, rs, to_seq, to_f):
        return pltpu.make_async_remote_copy(
            src_ref=src, dst_ref=dst, send_sem=ss, recv_sem=rs,
            device_id=(to_seq, to_f), device_id_type=MESH,
        )

    def rows_of(index):
        return pl.ds(pl.multiple_of(index * depth, depth), depth)

    loads = [
        pltpu.make_async_copy(w, wfull.at[rows_of(me), pl.ds(i * HDIM, HDIM)], load_sem.at[i])
        for i, w in enumerate((wq_hbm, wk_hbm, wv_hbm))
    ]
    loads.append(pltpu.make_async_copy(tok_hbm, tok, load_sem.at[3]))
    loads.append(pltpu.make_async_copy(mask_hbm, mask_ref, load_sem.at[4]))
    loads.append(pltpu.make_async_copy(gain_hbm, gain_ref, load_sem.at[5]))
    loads.append(pltpu.make_async_copy(cot_hbm, cot_ref, load_sem.at[6]))
    for c in loads:
        c.start()

    barrier = pltpu.get_barrier_semaphore()
    for t in range(1, nz):
        pl.semaphore_signal(
            barrier, inc=1, device_id=(2 * lax.rem(z + t, nz) + k, f), device_id_type=MESH
        )
    pl.semaphore_signal(barrier, inc=1, device_id=(other, f), device_id_type=MESH)
    for t in range(1, nf):
        pl.semaphore_signal(
            barrier, inc=1, device_id=(me, lax.rem(f + t, nf)), device_id_type=MESH
        )
    for c in loads[:3]:
        c.wait()
    pl.semaphore_wait(barrier, nz - 1 + 1 + nf - 1)

    part = depth // 2

    def part_of(index, u):
        return pl.ds(pl.multiple_of(index * depth + u * part, part), part)

    def w_right(s, u):
        r = part_of(2 * (z - s) + k, u)
        n = 2 * s + u
        return rcopy(wfull.at[r], wfull.at[r], w_rs.at[n], w_rr.at[n], 2 * (z + 1) + k, f)

    def w_left(s, u):
        r = part_of(2 * (z + s) + k, u)
        n = 2 * s + u
        return rcopy(wfull.at[r], wfull.at[r], w_ls.at[n], w_lr.at[n], 2 * (z - 1) + k, f)

    def w_pair(j, u):
        r = part_of(2 * j + k, u)
        n = 2 * j + u
        return rcopy(wfull.at[r], wfull.at[r], w_ps.at[n], w_pr.at[n], other, f)

    half = pl.ds(pl.multiple_of(k * depth, depth), depth)

    def w_across(j):
        return rcopy(
            wfull.at[rows_of(2 * j + k)], woth.at[f, half], wo_s.at[j], wo_r.at[f], me, j
        )

    def w_across_pair(j):
        return rcopy(woth.at[j, half], woth.at[j, half], wop_s.at[j], wop_r.at[j], other, f)

    def send_across(j):
        @pl.when(j != f)
        def _():
            w_across(j).start()

    def add_pair(j):
        for u in range(2):
            r = part_of(2 * j + 1 - k, u)
            n = 2 * j + u
            rcopy(wfull.at[r], wfull.at[r], w_ps.at[n], w_pr.at[n], other, f).wait_recv()
        span = pl.ds(pl.multiple_of(j * 2 * depth, 2 * depth), 2 * depth)
        proj[...] += mm(tok[:, span], wfull[span])

    def right_has(s):
        return (z < nz - 1) & (z >= s)

    def left_has(s):
        return (z > 0) & (z + s <= nz - 1)

    for u in range(2):
        @pl.when(z < nz - 1)
        def _():
            w_right(0, u).start()

        @pl.when(z > 0)
        def _():
            w_left(0, u).start()

    for u in range(2):
        w_pair(z, u).start()
    send_across(z)
    for c in loads[3:]:
        c.wait()
    tok_t[...] = tok[...].T
    row = lax.broadcasted_iota(jnp.int32, (seg, seg), 0)
    col = lax.broadcasted_iota(jnp.int32, (seg, seg), 1)
    zero = jnp.zeros((seg, seg), F32)
    total = jnp.where(col <= row, 1.0, zero)
    for a in range(NB):
        for b in range(a):
            inside = (
                (row >= a * BLOCK) & (row < (a + 1) * BLOCK)
                & (col >= b * BLOCK) & (col < (b + 1) * BLOCK)
            )
            m = jnp.where(mask_ref[a, 0:1, b : b + 1] == 1, 1.0, 0.0)
            total = jnp.where(inside, m, total)
    allow[...] = total
    proj[...] = jnp.zeros_like(proj)

    for s in range(nz - 1):
        for u in range(2):
            n = 2 * s + u

            @pl.when(z - 1 - s >= 0)
            def _():
                r = part_of(2 * (z - 1 - s) + k, u)
                rcopy(wfull.at[r], wfull.at[r], w_rs.at[n], w_rr.at[n], other, f).wait_recv()
                if s < nz - 2:
                    @pl.when(z < nz - 1)
                    def _():
                        w_right(s + 1, u).start()

                w_pair(z - 1 - s, u).start()
                if u == 1:
                    send_across(z - 1 - s)

            @pl.when(z + 1 + s <= nz - 1)
            def _():
                r = part_of(2 * (z + 1 + s) + k, u)
                rcopy(wfull.at[r], wfull.at[r], w_ls.at[n], w_lr.at[n], other, f).wait_recv()
                if s < nz - 2:
                    @pl.when(z > 0)
                    def _():
                        w_left(s + 1, u).start()

                w_pair(z + 1 + s, u).start()
                if u == 1:
                    send_across(z + 1 + s)

        if s == 0:
            add_pair(z)
        else:
            @pl.when(z - s >= 0)
            def _():
                add_pair(z - s)

            @pl.when(z + s <= nz - 1)
            def _():
                add_pair(z + s)

    @pl.when(z == nz - 1)
    def _():
        add_pair(0)

    @pl.when(z == 0)
    def _():
        add_pair(nz - 1)

    projected = proj[...].astype(BF)
    q = projected[:, :HDIM]
    key = projected[:, HDIM : 2 * HDIM]
    v = projected[:, 2 * HDIM :]

    def exchange_start(mine, out, inbox, pair_in, s_sem, r_sem, p_sem, backward):
        out[...] = mine.astype(BF)
        for t in range(1, nz):
            there = z - t if backward else z + t

            @pl.when((there >= 0) & (there < nz))
            def _():
                rcopy(
                    out, inbox.at[z], s_sem.at[t], r_sem.at[z], 2 * there + k, f
                ).start()

        @pl.when(k == (1 if backward else 0))
        def _():
            rcopy(out, pair_in, p_sem.at[0], p_sem.at[1], other, f).start()

    def exchange_wait(out, inbox, pair_in, t_out, t_in, acc, r_sem, p_sem, t_sem, backward):
        acc[...] = jnp.zeros_like(acc)
        for t in range(1, nz):
            there = z + t if backward else z - t

            @pl.when((there >= 0) & (there < nz))
            def _():
                rcopy(
                    out, inbox.at[there], p_sem.at[0], r_sem.at[there], other, f
                ).wait_recv()
                acc[...] += inbox[there].astype(F32)

        t_out[...] = acc[...].astype(BF)
        total = rcopy(t_out, t_in, t_sem.at[0], t_sem.at[1], other, f)
        total.start()

        @pl.when(k == (0 if backward else 1))
        def _():
            rcopy(out, pair_in, p_sem.at[0], p_sem.at[1], other, f).wait_recv()
            acc[...] += pair_in[...].astype(F32)

        total.wait()
        return (acc[...] + t_in[...].astype(F32)).astype(BF)

    def exchange_end(out, inbox, pair_in, s_sem, r_sem, p_sem, backward):
        for t in range(1, nz):
            there = z - t if backward else z + t

            @pl.when((there >= 0) & (there < nz))
            def _():
                rcopy(
                    out, inbox.at[z], s_sem.at[t], r_sem.at[z], 2 * there + k, f
                ).wait_send()

        @pl.when(k == (1 if backward else 0))
        def _():
            rcopy(out, pair_in, p_sem.at[0], p_sem.at[1], other, f).wait_send()

    exchange_start(mm_tn(key, v), inc_out, inc_in, inc_pair, st_s, st_r, stp, False)
    ok = allow[...]
    weights = (mm_nt(q, key) * ok).astype(BF)
    mixed = mm(weights, v)
    gain = gain_ref[...]
    given = cot_ref[...].astype(F32) * gain

    state = exchange_wait(inc_out, inc_in, inc_pair, tot_out, tot_in, run, st_r, stp, tp, False)
    mixed = mixed + mm(q, state)
    scale = lax.rsqrt(jnp.mean(mixed * mixed, axis=-1, keepdims=True) + EPSILON)
    normed = mixed * scale
    d_mixed = (
        scale * (given - normed * jnp.mean(given * normed, axis=-1, keepdims=True))
    ).astype(BF)
    exchange_start(mm_tn(q, d_mixed), dst_out, dst_in, dst_pair, ds_s, ds_r, dsp, True)
    att_ref[...] = (normed * gain).astype(BF)
    d_weights = (mm_nt(d_mixed, v) * ok).astype(BF)
    gq_own[...] = (mm_nt(d_mixed, state) + mm(d_weights, key)).astype(BF)

    def across(own, oth, s_sem, r_sem, t):
        there = lax.rem(f + t, nf)
        return rcopy(own, oth.at[f], s_sem.at[t], r_sem.at[f], me, there)

    def across_wait(own, oth, s_sem, r_sem, t):
        there = lax.rem(f + t, nf)
        rcopy(own, oth.at[there], s_sem.at[t], r_sem.at[there], other, f).wait_recv()
        return there

    order = []
    for i in range(nz):
        for j in (nz - 1 - i, i):
            if j not in order:
                order.append(j)

    def rs_start(g, ps, pr, p_s, p_r):
        grads = g[...]
        for j in order:
            ps[j] = mm(tok_t[rows_of(2 * j + 1 - k)], grads).astype(BF)
            rcopy(ps.at[j], pr.at[j], p_s.at[j], p_r.at[j], other, f).start()

    def rs_mine(g, mine):
        grads = g[...]
        for j in order:
            mine[j] = mm(tok_t[rows_of(2 * j + k)], grads)

    def rs_ends(ps, pr, cs, cr, cl, mine, p_s, p_r, c_s, c_r, l_s, l_r):
        @pl.when(z == 0)
        def _():
            for j in range(nz - 1, 0, -1):
                rcopy(ps.at[j], pr.at[j], p_s.at[j], p_r.at[j], other, f).wait_recv()
                cs[j] = (mine[j] + pr[j].astype(F32)).astype(BF)
                rcopy(cs.at[j], cr.at[j], c_s.at[j], c_r.at[j], 2 + k, f).start()

        @pl.when(z == nz - 1)
        def _():
            for j in range(nz - 1):
                rcopy(ps.at[j], pr.at[j], p_s.at[j], p_r.at[j], other, f).wait_recv()
                cs[j] = (mine[j] + pr[j].astype(F32)).astype(BF)
                rcopy(cs.at[j], cl.at[j], l_s.at[j], l_r.at[j], 2 * (nz - 2) + k, f).start()

    def rs_inner(ps, pr, cs, cr, cl, mine, p_s, p_r, c_s, c_r, l_s, l_r):
        for i in range(nz - 1):
            j = nz - 1 - i

            @pl.when((z < j) & (z > 0))
            def _():
                rcopy(ps.at[j], pr.at[j], p_s.at[j], p_r.at[j], other, f).wait_recv()
                mine[j] += pr[j].astype(F32)
                rcopy(cs.at[j], cr.at[j], c_s.at[j], c_r.at[j], other, f).wait_recv()
                cs[j] = (mine[j] + cr[j].astype(F32)).astype(BF)
                rcopy(cs.at[j], cr.at[j], c_s.at[j], c_r.at[j], 2 * (z + 1) + k, f).start()

            @pl.when((z > i) & (z < nz - 1))
            def _():
                rcopy(ps.at[i], pr.at[i], p_s.at[i], p_r.at[i], other, f).wait_recv()
                mine[i] += pr[i].astype(F32)
                rcopy(cs.at[i], cl.at[i], l_s.at[i], l_r.at[i], other, f).wait_recv()
                cs[i] = (mine[i] + cl[i].astype(F32)).astype(BF)
                rcopy(cs.at[i], cl.at[i], l_s.at[i], l_r.at[i], 2 * (z - 1) + k, f).start()

    def rs_end(ps, pr, cs, cr, cl, mine, p_s, p_r, c_s, c_r, l_s, l_r):
        rcopy(ps.at[z], pr.at[z], p_s.at[z], p_r.at[z], other, f).wait_recv()
        mine[z] += pr[z].astype(F32)

        @pl.when(z > 0)
        def _():
            rcopy(cs.at[z], cr.at[z], c_s.at[z], c_r.at[z], other, f).wait_recv()
            mine[z] += cr[z].astype(F32)

        @pl.when(z < nz - 1)
        def _():
            rcopy(cs.at[z], cl.at[z], l_s.at[z], l_r.at[z], other, f).wait_recv()
            mine[z] += cl[z].astype(F32)

        return mine[z] * (1.0 / math.sqrt(seg * 2 * nz))

    def rs_drain(ps, pr, cs, cr, cl, mine, p_s, p_r, c_s, c_r, l_s, l_r):
        for j in range(nz):
            rcopy(ps.at[j], pr.at[j], p_s.at[j], p_r.at[j], other, f).wait_send()

            @pl.when(z < j)
            def _():
                rcopy(cs.at[j], cr.at[j], c_s.at[j], c_r.at[j], other, f).wait_send()

            @pl.when(z > j)
            def _():
                rcopy(cs.at[j], cl.at[j], l_s.at[j], l_r.at[j], other, f).wait_send()

    q_set = (psq, prq, csq, crq, clq, mineq, pq_s, pq_r, cq_s, cq_r, lq_s, lq_r)
    k_set = (psk, prk, csk, crk, clk, minek, pk_s, pk_r, ck_s, ck_r, lk_s, lk_r)

    for t in range(1, nf):
        across(gq_own, gq_oth, gq_s, gq_r, t).start()
    rs_start(gq_own, psq, prq, pq_s, pq_r)
    for t in range(1, nf):
        there = lax.rem(f + t, nf)
        rcopy(
            wfull.at[rows_of(me)], woth.at[there, half], wo_s.at[there], wo_r.at[there], other, f
        ).wait_recv()
        w_across_pair(there).start()
    d_keys = mm_tn(d_weights, q)
    d_values = mm_tn(weights, d_mixed)
    rs_mine(gq_own, mineq)
    rs_ends(*q_set)

    later = exchange_wait(dst_out, dst_in, dst_pair, dtot_out, dtot_in, drun, ds_r, dsp, dtp, True)
    gkv_own[:, :HDIM] = (d_keys + mm_nt(v, later)).astype(BF)
    gkv_own[:, HDIM:] = (d_values + mm(key, later)).astype(BF)
    for t in range(1, nf):
        across(gkv_own, gkv_oth, gkv_s, gkv_r, t).start()
    rs_start(gkv_own, psk, prk, pk_s, pk_r)
    rs_mine(gkv_own, minek)
    rs_inner(*q_set)
    rs_ends(*k_set)
    rs_inner(*k_set)

    mine_rows = pl.ds(pl.multiple_of(f * 2 * depth, depth), 2 * depth)
    total = mm_nt(gq_own[...], wfull[mine_rows, :HDIM])
    total = total + mm_nt(gkv_own[...], wfull[mine_rows, HDIM:])
    away = pl.ds(pl.multiple_of((1 - k) * depth, depth), depth)
    for t in range(1, nf):
        there = lax.rem(f + t, nf)
        rcopy(
            woth.at[there, away], woth.at[there, away], wop_s.at[there], wop_r.at[there], other, f
        ).wait_recv()
        across_wait(gq_own, gq_oth, gq_s, gq_r, t)
        across_wait(gkv_own, gkv_oth, gkv_s, gkv_r, t)
        total = total + mm_nt(gq_oth[there], woth[there, :, :HDIM])
        total = total + mm_nt(gkv_oth[there], woth[there, :, HDIM:])
    gt_ref[...] = total.astype(BF)

    gq_ref[...] = rs_end(*q_set).astype(BF)
    both = rs_end(*k_set)
    gk_ref[...] = both[:, :HDIM].astype(BF)
    gv_ref[...] = both[:, HDIM:].astype(BF)

    for s in range(nz - 1):
        @pl.when(right_has(s))
        def _():
            for u in range(2):
                w_right(s, u).wait_send()

        @pl.when(left_has(s))
        def _():
            for u in range(2):
                w_left(s, u).wait_send()

    for j in range(nz):
        for u in range(2):
            w_pair(j, u).wait_send()

        @pl.when(f != j)
        def _():
            w_across(j).wait_send()
            w_across_pair(j).wait_send()

    exchange_end(inc_out, inc_in, inc_pair, st_s, st_r, stp, False)
    exchange_end(dst_out, dst_in, dst_pair, ds_s, ds_r, dsp, True)
    for t in range(1, nf):
        across(gq_own, gq_oth, gq_s, gq_r, t).wait_send()
        across(gkv_own, gkv_oth, gkv_s, gkv_r, t).wait_send()
    rs_drain(*q_set)
    rs_drain(*k_set)


def shards(nz, nf, tokens, w_query, w_key, w_value, norm_gain, block_mask, cotangent):
    seg, features = tokens.shape
    depth, columns = w_query.shape
    vm = pl.BlockSpec(memory_space=pltpu.VMEM)
    hbm = pl.BlockSpec(memory_space=pl.ANY)
    dma = pltpu.SemaphoreType.DMA
    wide = 3 * columns

    def buf(*shape, kind=BF):
        return pltpu.VMEM(shape, kind)

    def exchange_bufs():
        return [
            buf(HDIM, HDIM), buf(nz, HDIM, HDIM), buf(HDIM, HDIM),
            buf(HDIM, HDIM), buf(HDIM, HDIM), buf(HDIM, HDIM, kind=F32),
        ]

    def rs_bufs(width):
        return [buf(nz, depth, width) for _ in range(5)] + [buf(nz, depth, width, kind=F32)]

    one = dma((nz,))
    exchange_sems = [dma((nz,)), dma((nz,)), dma((2,)), dma((2,))]
    scratch = (
        [
            buf(seg, features), buf(features, seg), buf(features, wide),
            buf(nf, 2 * depth, wide), buf(seg, seg, kind=F32),
            buf(seg, wide, kind=F32), buf(1, columns, kind=F32),
            buf(NB, 1, NB, kind=jnp.int32), buf(seg, columns),
        ]
        + exchange_bufs() + exchange_bufs()
        + [
            buf(seg, HDIM), buf(seg, 2 * HDIM),
            buf(nf, seg, HDIM), buf(nf, seg, 2 * HDIM),
        ]
        + rs_bufs(HDIM) + rs_bufs(2 * HDIM)
        + [dma((7,))] + [dma((2 * nz,))] * 6 + [ dma((nf,)), dma((nf,)), dma((nf,)), dma((nf,))]
        + exchange_sems + exchange_sems
        + [dma((nf,))] * 4
        + [one] * 12
    )
    return pl.pallas_call(
        functools.partial(kernel, nz, nf),
        out_shape=(
            jax.ShapeDtypeStruct((seg, columns), BF),
            jax.ShapeDtypeStruct((seg, features // nf), BF),
            jax.ShapeDtypeStruct((depth, columns), BF),
            jax.ShapeDtypeStruct((depth, columns), BF),
            jax.ShapeDtypeStruct((depth, columns), BF),
        ),
        in_specs=[hbm] * 7,
        out_specs=(vm,) * 5,
        scratch_shapes=scratch,
        compiler_params=pltpu.CompilerParams(
            collective_id=0, has_side_effects=True, vmem_limit_bytes=LIMIT
        ),
    )(
        tokens, w_query, w_key, w_value, norm_gain.reshape(1, columns),
        jnp.transpose(block_mask, (1, 0, 2)), cotangent
    )


def solution(mesh):
    nz, nf = mesh.shape["seq"] // 2, mesh.shape["fsdp"]
    assert nz == nf
    placed = (
        P("seq", None),
        P("seq", "fsdp"),
        P("seq", "fsdp"),
        P("seq", "fsdp"),
        P("fsdp"),
        P("seq", None, None),
        P("seq", "fsdp"),
    )
    return jax.shard_map(
        functools.partial(shards, nz, nf),
        mesh=mesh,
        in_specs=placed,
        out_specs=(P("seq", "fsdp"),) * 5,
        check_vma=False,
    )
```
